256 devices in a mesh: lon: 64 (over y_lo, z, x), grp: 4 (over y_hi, core).
Axes of the slice: x: 4, y: 4 (y_hi: 2, y_lo: 2; y = y_hi * 2 + y_lo), z: 8, core: 2. Of those that a mesh axis runs over, the one named last changes fastest.
Arguments:
- left_feat: bfloat16 [320, 512, 128], P('grp', 'lon'), may hold values from -6 to 6
- right_feat: bfloat16 [320, 512, 128], P('grp', 'lon'), may hold values from -6 to 6
- conv_cot: bfloat16 [48, 32, 512, 128], P('grp', None, 'lon'), may hold values from -6 to 6
- conv_weight: bfloat16 [32, 40, 3, 3, 3], replicated, may hold values from -0.1875 to 0.1875
- disparity_shift: int32 [512, 128], P('lon'), may hold values from 0 to 47
- valid_mask: int32 [512, 128], P('lon'), may hold values 0 or 1
Outputs:
- left_grad: float32 [320, 512, 128], P('grp', 'lon')
- right_grad: float32 [320, 512, 128], P('grp', 'lon')
- weight_grad: float32 [32, 40, 3, 3, 3], replicated
The draws below stay inside these ranges and needn't reach their ends.
Inputs may be any that keep to these rules, and one draw needn't show every extreme that they name: `disparity_shift`: a column shift of the right features.
All inputs are finite; a program needn't handle non-finite values. No bound on the sum of `valid_mask` on one device may be relied on, other than what follows from the above.
Results may differ from the reference program's by a relative error of at most 0.0032.
Values may be sent and summed in bfloat16 or wider, within the bound.
No kernel may reach another device: no remote copies, remote signals or barrier semaphores. Data moves between devices by JAX's collectives and lax.ppermute only.
A program may use at most 192 MiB of HBM per device.

```python
import math
import jax
import jax.numpy as jnp
from jax import lax

C_FEAT = 320
GROUPS = 40
CG = 8
OUTC = 32
DISP = 48
HWIN = 128
COLS = 512


def plant(drawn, key, least, largest):
    index_at = [jax.random.randint(jax.random.fold_in(key, axis), (), 0, length) for axis, length in enumerate(drawn.shape)]
    longest = drawn.shape.index(max(drawn.shape))
    beside = index_at[:longest] + [(index_at[longest] + 1) % drawn.shape[longest]] + index_at[longest + 1:]
    return drawn.at[tuple(index_at)].set(least).at[tuple(beside)].set(largest)


def block_levels(key, extent, shards, smallest, largest):
    gain = 1.0
    for dim, parts in shards:
        draws = jax.random.uniform(jax.random.fold_in(jax.random.fold_in(key, 6), dim), (parts,), jnp.float32, smallest / len(shards), largest / len(shards))
        gain = gain * jnp.repeat(jnp.exp(draws), extent[dim] // parts).reshape((-1,) + (1,) * (len(extent) - 1 - dim))
    return gain


def gaussian(own_key, shape, spread, bound, shards=(), kind=jnp.bfloat16):
    level = block_levels(own_key, shape, shards, -0.22, 0.18) if shards else 1.0
    drawn = jax.random.normal(own_key, shape, jnp.float32) * spread * level
    return jnp.minimum(jnp.maximum(drawn, -bound), bound).astype(kind)


def setup_inputs(seed: int = 0) -> dict:
    splits = jax.random.split(jax.random.key(seed), 7)
    left_feat = gaussian(splits[0], (C_FEAT, COLS, HWIN), 1.0, 6.0, ((0, 4), (1, 64)))
    right_feat = gaussian(splits[1], (C_FEAT, COLS, HWIN), 1.0, 6.0, ((0, 4), (1, 64)))
    conv_cot = gaussian(splits[2], (DISP, OUTC, COLS, HWIN), 1.0, 6.0, ((0, 4), (2, 64)))
    conv_weight = gaussian(splits[3], (OUTC, GROUPS, 3, 3, 3), (GROUPS * 27) ** -0.5, 0.1875)
    disparity_shift = plant(jax.random.randint(splits[4], (COLS, HWIN), 0, DISP), jax.random.fold_in(splits[4], 1), 0, DISP - 1).astype(jnp.int32)
    valid_mask = plant((jax.random.randint(splits[5], (COLS, HWIN), 0, 4) < 3).astype(jnp.int32), jax.random.fold_in(splits[5], 1), 0, 1)
    return {"left_feat": left_feat, "right_feat": right_feat, "conv_cot": conv_cot, "conv_weight": conv_weight, "disparity_shift": disparity_shift, "valid_mask": valid_mask}


photo_weight = 0.5

def conv_forward(volume, kernel):
    wrapped = jnp.concatenate([volume[:, :, -2:, :], volume, volume[:, :, :2, :]], axis=2)
    result = lax.conv_general_dilated(wrapped[None], kernel, window_strides=(1, 1, 1), padding=((2, 2), (0, 0), (2, 2)), rhs_dilation=(2, 2, 2), dimension_numbers=('NDCWH', 'OIDWH', 'NDCWH'), precision=lax.Precision.HIGHEST)
    return result[0]

def reference(left_feat, right_feat, conv_cot, conv_weight, disparity_shift, valid_mask):
    left_wide = left_feat.astype(jnp.float32)
    right_wide = right_feat.astype(jnp.float32)

    def cost_of(disparity):
        shifted = jnp.roll(right_wide, disparity, axis=1)
        return lax.optimization_barrier(jnp.sum((left_wide * shifted).reshape(GROUPS, CG, COLS, HWIN), axis=1)) / CG
    volume = lax.map(cost_of, jnp.arange(DISP, dtype=jnp.int32)).astype(jnp.bfloat16)
    outputs, pullback = jax.vjp(conv_forward, volume.astype(jnp.float32), conv_weight.astype(jnp.float32))
    grad_volume, grad_kernel = pullback(conv_cot.astype(jnp.float32))
    grad_cost = grad_volume.astype(jnp.bfloat16)
    weight_grad = grad_kernel * (1.0 / math.sqrt(DISP * COLS * HWIN))
    source_column = (jnp.arange(COLS, dtype=jnp.int32)[:, None] - disparity_shift) % COLS
    warped = jnp.take_along_axis(right_wide, jnp.broadcast_to(source_column[None], right_wide.shape), axis=1)
    residual = valid_mask.astype(jnp.float32) * (left_wide - warped)

    def accumulate(running, disparity):
        left_run, right_run = running
        weight = jnp.repeat(grad_cost[disparity].astype(jnp.float32), CG, axis=0) / CG
        shifted = jnp.roll(right_wide, disparity, axis=1)
        chosen = (disparity_shift == disparity).astype(jnp.float32)
        gradient_term = weight * left_wide - photo_weight * chosen * residual
        return ((left_run + weight * shifted, right_run + jnp.roll(gradient_term, -disparity, axis=1)), None)
    start_pair = (photo_weight * residual, jnp.zeros(right_wide.shape, jnp.float32))
    final_pair = lax.scan(accumulate, start_pair, jnp.arange(DISP, dtype=jnp.int32))[0]
    return (final_pair[0], final_pair[1], weight_grad)
```

```python
import functools
import math

import jax
import jax.numpy as jnp
import numpy as np
from jax import lax
from jax.experimental import pallas as pl
from jax.experimental.pallas import tpu as pltpu
from jax.sharding import PartitionSpec as P

CG = 8
DISP = 48
OUTC = 32
COLS_HERE = 8
BLOCKS = 7
ROWS = 384
F32 = jnp.float32
BF16 = jnp.bfloat16
MIB = 1024 * 1024


def filter_column():
    index = np.arange(ROWS)
    own, left = index < 256, index < 320
    column = np.where(own, index % 8, np.where(left, index % 2 - 2, index % 2 + 8))
    channel = np.where(own, index // 8, np.where(left, (index - 256) // 2, (index - 320) // 2))
    return column, channel


def plane_copies(rank, own, halo, planes, first, sems):
    copies = []
    for k in range(4):
        start = (rank ^ k) * 12 + first
        copies.append(
            pltpu.make_async_copy(
                own[k], planes.at[pl.ds(start, 12), pl.ds(0, 256)], sems.at[k]
            )
        )
        copies.append(
            pltpu.make_async_copy(
                halo[k], planes.at[pl.ds(start, 12), pl.ds(256, 128)], sems.at[4 + k]
            )
        )
    return copies


def conv_kernel(rank_ref, kernel_ref, *refs):
    own, halo = refs[0:4], refs[4:8]
    out_ref, planes, sems = refs[8:]
    copies = plane_copies(rank_ref[0], own, halo, planes, 2, sems)
    for copy in copies:
        copy.start()
    planes[0:2] = jnp.zeros((2, ROWS, 128), BF16)
    planes[50:52] = jnp.zeros((2, ROWS, 128), BF16)
    for copy in copies:
        copy.wait()
    lane = lax.broadcasted_iota(jnp.int32, (80, 128), 1)

    def pair(index, carry):
        d = index * 2
        parts = []
        for a in range(3):
            parts.append(
                jnp.concatenate([planes[d + 4 - 2 * a], planes[d + 5 - 2 * a]], axis=1)
            )
        columns = jnp.concatenate(parts, axis=0)
        product = jnp.dot(kernel_ref[...], columns, preferred_element_type=F32)
        for half in range(2):
            part = product[:, half * 128 : half * 128 + 128]
            ahead = jnp.where(lane < 126, pltpu.roll(part[0:80], 126, 1), 0.0)
            behind = jnp.where(lane >= 2, pltpu.roll(part[160:240], 2, 1), 0.0)
            out_ref[d + half] = (part[80:160] + ahead + behind).astype(BF16)
        return carry

    lax.fori_loop(0, 24, pair, 0)


def rolled(value, steps, axis):
    return value if steps == 0 else pltpu.roll(value, steps, axis)


def widen(left_ref, panels, left_rolls, wide):
    def two(index, carry):
        rows = pl.ds(pl.multiple_of(index * 16, 16), 16)
        value = left_ref[rows, :].astype(F32)
        for half in range(2):
            part = value[half * 8 : half * 8 + 8]
            place = pl.ds(pl.multiple_of(index * 16 + half * 8, 8), 8)
            for r in range(8):
                left_rolls[r, place, :] = rolled(part, (8 - r) % 8, 0)
        for b in range(BLOCKS):
            wide[b, rows, :] = panels[b][rows, :].astype(F32)
        return carry

    lax.fori_loop(0, 40, two, 0)


def cost_kernel(rank_ref, left_ref, *refs):
    panels = refs[0:7]
    own, halo = refs[7:11], refs[11:15]
    mask_ref, sum_ref, out_ref, left_rolls, wide, planes, volume, total, sems = refs[15:]
    copies = plane_copies(rank_ref[0], own, halo, planes, 0, sems)
    for copy in copies:
        copy.start()
    widen(left_ref, panels, left_rolls, wide)
    volume[0:2] = jnp.zeros((2, 240, 128), BF16)
    volume[50:52] = jnp.zeros((2, 240, 128), BF16)
    row = lax.broadcasted_iota(jnp.int32, (8, 128), 0)
    lane = lax.broadcasted_iota(jnp.int32, (16, 128), 1)

    def groups(index, carry):
        base = index * 128
        for r in range(8):
            sums = []
            for half in range(2):
                line = []
                for b in range(BLOCKS):
                    acc = None
                    for c in range(CG):
                        place = pl.ds(pl.multiple_of(base + half * 64 + c * 8, 8), 8)
                        term = left_rolls[r, place, :] * wide[b, place, :]
                        acc = term if acc is None else acc + term
                    line.append(acc)
                sums.append(line)
            for q in range(6):
                both = []
                for half in range(2):
                    line = sums[half]
                    mixed = jnp.where(row <= 7 - r, line[6 - q], line[5 - q]) if r else line[6 - q]
                    both.append(rolled(mixed, r, 0))
                cost = jnp.concatenate(both, axis=0) * (1.0 / CG)
                d = 8 * q + r
                later = jnp.where(lane >= 2, pltpu.roll(cost, 2, 1), 0.0)
                sooner = jnp.where(lane < 126, pltpu.roll(cost, 126, 1), 0.0)
                for e, value in enumerate((later, cost, sooner)):
                    place = pl.ds(pl.multiple_of(e * 80 + index * 16, 16), 16)
                    volume[d + 2, place, :] = value.astype(BF16)
        return carry

    lax.fori_loop(0, 5, groups, 0)
    for copy in copies:
        copy.wait()
    total[...] = jnp.zeros_like(total)

    def chunk(index, carry):
        d = index * 8
        cot = jnp.concatenate([planes[d + j] for j in range(8)], axis=1)
        for a in range(3):
            cost = jnp.concatenate([volume[d + j + 2 * a] for j in range(8)], axis=1)
            total[a] += lax.dot_general(
                cost, cot, (((1,), (1,)), ((), ())), preferred_element_type=F32
            )
        return carry

    lax.fori_loop(0, 6, chunk, 0)
    out_ref[...] = jnp.zeros_like(out_ref)
    for a in range(3):
        terms = total[a].reshape(30, 8, ROWS)
        for b in range(3):
            picked = jnp.sum(terms * mask_ref[b][None], axis=1)
            out_ref[a * 32 : a * 32 + 30, b * 32 : b * 32 + 32] = jnp.dot(
                picked, sum_ref[...], preferred_element_type=F32, precision=lax.Precision.HIGHEST
            )


def grad_kernel(left_ref, *refs):
    panels = refs[0:7]
    grad_ref, shift_ref, valid_ref = refs[7:10]
    left_out, right_out = refs[10], refs[11:18]
    left_rolls, wide, chosen, counts, weights = refs[18:]
    widen(left_ref, panels, left_rolls, wide)
    row = lax.broadcasted_iota(jnp.int32, (8, 128), 0)
    valid = valid_ref[...].astype(F32)
    shift = shift_ref[...]
    for r in range(8):
        shift_r = rolled(shift, (8 - r) % 8, 0)
        valid_r = rolled(valid, (8 - r) % 8, 0)
        for b in range(BLOCKS):
            q = 6 - b
            at = jnp.where(row <= 7 - r, 8 * q + r, 8 * (q - 1) + r)
            chosen[b, r] = jnp.where(shift_r == at, valid_r, 0.0)
    for b in range(BLOCKS):
        count = chosen[b, 0]
        for r in range(1, 8):
            count = count + chosen[b, r]
        counts[b] = 0.5 * count

    def groups(index, carry):
        pair_rows = pl.ds(pl.multiple_of(index * 16, 16), 16)
        for r in range(8):
            lines = [[], []]
            for q in range(6):
                value = grad_ref[8 * q + r, pair_rows, :].astype(F32)
                for half in range(2):
                    lines[half].append(rolled(value[half * 8 : half * 8 + 8], (8 - r) % 8, 0))
            for half in range(2):
                for b in range(BLOCKS):
                    low = lines[half][6 - b] if b > 0 else 0.0
                    high = lines[half][5 - b] if b < 6 else 0.0
                    mixed = jnp.where(row <= 7 - r, low, high)
                    weights[half, b, r] = mixed * (1.0 / CG) - 0.5 * chosen[b, r]
        base = index * 128
        for half in range(2):
            for b in range(BLOCKS):
                factors = [weights[half, b, r] for r in range(8)]
                count = counts[b]
                for c in range(0, CG, 2):
                    both = []
                    for k in range(2):
                        place = pl.ds(pl.multiple_of(base + half * 64 + (c + k) * 8, 8), 8)
                        acc = count * wide[b, place, :]
                        for r in range(8):
                            acc = acc + factors[r] * left_rolls[r, place, :]
                        both.append(acc)
                    place = pl.ds(pl.multiple_of(base + half * 64 + c * 8, 16), 16)
                    right_out[b][place, :] = jnp.concatenate(both, axis=0).astype(
                        right_out[b].dtype
                    )
            sums = []
            for c in range(CG):
                place = pl.ds(pl.multiple_of(base + half * 64 + c * 8, 8), 8)
                sums.append(0.5 * valid * left_rolls[0, place, :])
            for r in range(8):
                factors = [weights[half, b, r] for b in range(BLOCKS)]
                for c in range(CG):
                    place = pl.ds(pl.multiple_of(base + half * 64 + c * 8, 8), 8)
                    acc = factors[0] * wide[0, place, :]
                    for b in range(1, BLOCKS):
                        acc = acc + factors[b] * wide[b, place, :]
                    sums[c] = sums[c] + rolled(acc, r, 0)
            for c in range(CG):
                place = pl.ds(pl.multiple_of(base + half * 64 + c * 8, 8), 8)
                left_out[place, :] = sums[c]
        return carry

    lax.fori_loop(0, 5, groups, 0)


SMEM = pl.BlockSpec(memory_space=pltpu.SMEM)
VMEM = pl.BlockSpec(memory_space=pltpu.VMEM)
ANY = pl.BlockSpec(memory_space=pl.ANY)


def run_conv(rank, kernel, own, halo):
    return pl.pallas_call(
        conv_kernel,
        out_shape=jax.ShapeDtypeStruct((DISP, 80, 128), BF16),
        in_specs=[SMEM, VMEM] + [ANY] * 8,
        out_specs=VMEM,
        scratch_shapes=[pltpu.VMEM((52, ROWS, 128), BF16), pltpu.SemaphoreType.DMA((8,))],
        compiler_params=pltpu.CompilerParams(vmem_limit_bytes=20 * MIB),
        cost_estimate=pl.CostEstimate(flops=15_000_000_000, bytes_accessed=8_000_000, transcendentals=0),
        name="filter_transpose",
    )(rank, kernel, *own, *halo)


def run_cost(rank, left, panels, own, halo):
    column, channel = filter_column()
    w = np.arange(8)[None, :, None]
    b = np.arange(3)[:, None, None]
    mask = (w == column[None, None, :] + 2 * b - 2).astype(np.float32)
    summing = (channel[:, None] == np.arange(OUTC)[None]).astype(np.float32)
    return pl.pallas_call(
        cost_kernel,
        out_shape=jax.ShapeDtypeStruct((96, 128), F32),
        in_specs=[SMEM, VMEM] + [VMEM] * 7 + [ANY] * 8 + [VMEM] * 2,
        out_specs=VMEM,
        scratch_shapes=[
            pltpu.VMEM((8, 640, 128), F32),
            pltpu.VMEM((BLOCKS, 640, 128), F32),
            pltpu.VMEM((DISP, ROWS, 128), BF16),
            pltpu.VMEM((52, 240, 128), BF16),
            pltpu.VMEM((3, 240, ROWS), F32),
            pltpu.SemaphoreType.DMA((8,)),
        ],
        compiler_params=pltpu.CompilerParams(vmem_limit_bytes=32 * MIB),
        cost_estimate=pl.CostEstimate(flops=15_000_000_000, bytes_accessed=8_000_000, transcendentals=0),
        name="cost_and_filter_grad",
    )(rank, left, *panels, *own, *halo, jnp.asarray(mask), jnp.asarray(summing))


def run_grad(left, panels, grad_cost, shift, valid):
    return pl.pallas_call(
        grad_kernel,
        out_shape=[jax.ShapeDtypeStruct((640, 128), F32)]
        + [jax.ShapeDtypeStruct((640, 128), BF16)] * 6
        + [jax.ShapeDtypeStruct((640, 128), F32)],
        in_specs=[VMEM] * 11,
        out_specs=[VMEM] * 8,
        scratch_shapes=[
            pltpu.VMEM((8, 640, 128), F32),
            pltpu.VMEM((BLOCKS, 640, 128), F32),
            pltpu.VMEM((BLOCKS, 8, 8, 128), F32),
            pltpu.VMEM((BLOCKS, 8, 128), F32),
            pltpu.VMEM((2, BLOCKS, 8, 8, 128), F32),
        ],
        compiler_params=pltpu.CompilerParams(vmem_limit_bytes=32 * MIB),
        cost_estimate=pl.CostEstimate(flops=8_000_000_000, bytes_accessed=4_000_000, transcendentals=0),
        name="feature_grads",
    )(left, *panels, grad_cost, shift, valid)


def conv_matrix(conv_weight, rank):
    column, channel = filter_column()
    local = lax.dynamic_slice_in_dim(conv_weight, rank * 10, 10, axis=1)
    taps = local.transpose(4, 1, 2, 3, 0)
    spread = (np.arange(OUTC)[:, None] == channel[None]).astype(np.float32)
    placed = jnp.einsum(
        "egabo,oc->egabc", taps, jnp.asarray(spread, BF16), preferred_element_type=BF16
    )
    w = np.arange(8)[None, :, None]
    b = np.arange(3)[:, None, None]
    fits = column[None, None, :] == w - 2 * b + 2
    total = None
    for tap in range(3):
        term = jnp.where(
            jnp.asarray(fits[tap])[None, None, :, None, :], placed[:, :, None, :, tap, :], 0
        )
        total = term if total is None else total + term
    return total.reshape(240, 3 * ROWS).astype(BF16)


def moved(value, axis, place):
    pairs = [(i, place(i)) for i in range(lax.axis_size(axis))]
    return lax.ppermute(value, axis, pairs)


def along(value, steps):
    count = lax.axis_size("lon")
    return moved(value, "lon", lambda i: (i + steps) % count)


def across(value, bits):
    return moved(value, "grp", lambda i: i ^ bits)


def summed_over_lon(value):
    total = value
    for k in range(1, 4):
        total = total + moved(value, "lon", lambda i: i - i % 4 + (i + k) % 4)
    value = total
    for k in range(1, 8):
        total = total + moved(value, "lon", lambda i: i - i % 32 + (i + 4 * k) % 32)
    return total + moved(total, "lon", lambda i: i ^ 32)


def shards(left_feat, right_feat, conv_cot, conv_weight, disparity_shift, valid_mask):
    rank = lax.axis_index("grp")
    rank_array = rank.astype(jnp.int32).reshape(1)
    panels = [along(right_feat, k).reshape(640, 128) for k in range(6, 0, -1)]
    panels.append(right_feat.reshape(640, 128))
    left = left_feat.reshape(640, 128)

    own = conv_cot.reshape(12, 256, 128)
    own_far = across(own, 2)
    before = along(conv_cot[:, :, 6:].reshape(12, 64, 128), 1)
    after = along(conv_cot[:, :, :2].reshape(12, 64, 128), -1)
    halo = jnp.concatenate([before, after], axis=1)
    halo_far = across(halo, 2)
    owns = [own, across(own, 1), own_far, across(own_far, 1)]
    halos = [halo, across(halo, 1), halo_far, across(halo_far, 1)]

    grad_cost = run_conv(rank_array, conv_matrix(conv_weight, rank), owns, halos)
    filter_part = run_cost(rank_array, left, panels, owns, halos)
    outs = run_grad(left, panels, grad_cost, disparity_shift, valid_mask)
    left_grad = outs[0].reshape(80, 8, 128)
    right_grad = outs[7]
    for k in range(1, 7):
        right_grad = right_grad + along(outs[1 + 6 - k], -k).astype(F32)
    right_grad = right_grad.reshape(80, 8, 128)

    total = summed_over_lon(filter_part)
    pieces = [total] + [across(total, k) for k in range(1, 4)]
    odd, high = (rank & 1) == 1, (rank & 2) == 2
    pieces = [jnp.where(odd, pieces[k ^ 1], pieces[k]) for k in range(4)]
    pieces = [jnp.where(high, pieces[k ^ 2], pieces[k]) for k in range(4)]
    scale = 1.0 / math.sqrt(DISP * 8 * lax.axis_size("lon") * 128)
    whole = jnp.stack(pieces)[:, :, :96].reshape(4, 3, 32, 3, OUTC)[:, :, :30]
    whole = whole.reshape(4, 3, 3, 10, 3, OUTC) * scale
    weight_grad = whole.transpose(5, 0, 3, 1, 4, 2).reshape(OUTC, 40, 3, 3, 3)
    return (left_grad, right_grad, weight_grad)


def solution(mesh):
    placed = (
        P("grp", "lon", None),
        P("grp", "lon", None),
        P("grp", None, "lon", None),
        P(),
        P("lon", None),
        P("lon", None),
    )
    return jax.shard_map(
        shards,
        mesh=mesh,
        in_specs=placed,
        out_specs=(P("grp", "lon", None), P("grp", "lon", None), P()),
        check_vma=False,
    )
```

```python
import functools
import math

import jax
import jax.numpy as jnp
import numpy as np
from jax import lax
from jax.experimental import pallas as pl
from jax.experimental.pallas import tpu as pltpu
from jax.sharding import PartitionSpec as P

CG = 8
DISP = 48
OUTC = 32
COLS_HERE = 8
BLOCKS = 7
ROWS = 384
F32 = jnp.float32
BF16 = jnp.bfloat16
MIB = 1024 * 1024


def filter_column():
    index = np.arange(ROWS)
    own, left = index < 256, index < 320
    column = np.where(own, index % 8, np.where(left, index % 2 - 2, index % 2 + 8))
    channel = np.where(own, index // 8, np.where(left, (index - 256) // 2, (index - 320) // 2))
    return column, channel


SLABS = 8


class PlaneLoad:
    def __init__(self, rank, slabs, planes, first, sems):
        self.copies = []
        for k in range(4):
            place = pl.ds((rank ^ k) * 12 + first, 12)
            for part, (row, rows) in enumerate(((0, 256), (256, 128))):
                self.copies.append(
                    pltpu.make_async_copy(
                        slabs[4 * part + k],
                        planes.at[place, pl.ds(row, rows)],
                        sems.at[4 * part + k],
                    )
                )

    def start(self):
        for copy in self.copies:
            copy.start()

    def wait(self):
        for copy in self.copies:
            copy.wait()


def transposed_filter(kernel_ref, planes, emit, unroll):
    lane = lax.broadcasted_iota(jnp.int32, (80, 128), 1)

    def pair(index, carry):
        d = index * 2
        parts = []
        for a in range(3):
            parts.append(
                jnp.concatenate([planes[d + 4 - 2 * a], planes[d + 5 - 2 * a]], axis=1)
            )
        columns = jnp.concatenate(parts, axis=0)
        product = jnp.dot(kernel_ref[...], columns, preferred_element_type=F32)
        for half in range(2):
            part = product[:, half * 128 : half * 128 + 128]
            ahead = jnp.where(lane < 126, pltpu.roll(part[0:80], 126, 1), 0.0)
            behind = jnp.where(lane >= 2, pltpu.roll(part[160:240], 2, 1), 0.0)
            emit(d + half, part[80:160] + ahead + behind)
        return carry

    lax.fori_loop(0, 24, pair, 0, unroll=unroll)


def conv_kernel(rank_ref, kernel_ref, *refs):
    slabs, (out_ref, planes, sems) = refs[0:SLABS], refs[SLABS:]
    load = PlaneLoad(rank_ref[0], slabs, planes, 2, sems)
    load.start()
    planes[0:2] = jnp.zeros((2, ROWS, 128), BF16)
    planes[50:52] = jnp.zeros((2, ROWS, 128), BF16)
    load.wait()

    def emit(d, value):
        out_ref[d] = value.astype(BF16)

    transposed_filter(kernel_ref, planes, emit, 4)


def rolled(value, steps, axis):
    return value if steps == 0 else pltpu.roll(value, steps, axis)


PANELS = 6


def panel_places(refs):
    one, two, three, four, pair, own = refs
    return [(pair, 640), (pair, 0), (four, 0), (three, 0), (two, 0), (one, 0), (own, 0)]


def widen(left_ref, panels, left_rolls, wide):
    def two(index, carry):
        rows = pl.ds(pl.multiple_of(index * 16, 16), 16)
        value = left_ref[rows, :].astype(F32)
        for half in range(2):
            part = value[half * 8 : half * 8 + 8]
            place = pl.ds(pl.multiple_of(index * 16 + half * 8, 8), 8)
            for r in range(8):
                left_rolls[r, place, :] = rolled(part, (8 - r) % 8, 0)
        for b in range(BLOCKS):
            panel, first = panels[b]
            there = pl.ds(pl.multiple_of(first + index * 16, 16), 16)
            value = panel[there, :].astype(F32)
            wide[b, rows, :] = value
        return carry

    lax.fori_loop(0, 40, two, 0)


def cost_kernel(left_ref, *refs):
    panels = panel_places(refs[0:PANELS])
    volume, left_rolls, wide = refs[PANELS:]
    widen(left_ref, panels, left_rolls, wide)
    volume[0:2] = jnp.zeros((2, 240, 128), BF16)
    volume[50:52] = jnp.zeros((2, 240, 128), BF16)
    row = lax.broadcasted_iota(jnp.int32, (8, 128), 0)
    lane = lax.broadcasted_iota(jnp.int32, (16, 128), 1)

    def groups(index, carry):
        base = index * 128
        for r in range(8):
            sums = []
            for half in range(2):
                line = []
                for b in range(BLOCKS):
                    acc = None
                    for c in range(CG):
                        place = pl.ds(pl.multiple_of(base + half * 64 + c * 8, 8), 8)
                        term = left_rolls[r, place, :] * wide[b, place, :]
                        acc = term if acc is None else acc + term
                    line.append(acc)
                sums.append(line)
            for q in range(6):
                both = []
                for half in range(2):
                    line = sums[half]
                    mixed = jnp.where(row <= 7 - r, line[6 - q], line[5 - q]) if r else line[6 - q]
                    both.append(rolled(mixed, r, 0))
                cost = jnp.concatenate(both, axis=0) * (1.0 / CG)
                d = 8 * q + r
                later = jnp.where(lane >= 2, pltpu.roll(cost, 2, 1), 0.0)
                sooner = jnp.where(lane < 126, pltpu.roll(cost, 126, 1), 0.0)
                for e, value in enumerate((later, cost, sooner)):
                    place = pl.ds(pl.multiple_of(e * 80 + index * 16, 16), 16)
                    volume[d + 2, place, :] = value.astype(BF16)
        return carry

    lax.fori_loop(0, 5, groups, 0)

def filter_kernel(rank_ref, volume, mask_ref, sum_ref, *refs):
    slabs, (out_ref, planes, total, sems) = refs[0:SLABS], refs[SLABS:]
    load = PlaneLoad(rank_ref[0], slabs, planes, 0, sems)
    load.start()
    total[...] = jnp.zeros_like(total)
    load.wait()

    def chunk(index, carry):
        d = index * 16
        cot = jnp.concatenate([planes[d + j] for j in range(16)], axis=1)
        for a in range(3):
            cost = jnp.concatenate([volume[d + j + 2 * a] for j in range(16)], axis=1)
            total[a] += lax.dot_general(
                cost, cot, (((1,), (1,)), ((), ())), preferred_element_type=F32
            )
        return carry

    lax.fori_loop(0, DISP // 16, chunk, 0)
    out_ref[...] = jnp.zeros_like(out_ref)
    for a in range(3):
        terms = total[a].reshape(30, 8, ROWS)
        for b in range(3):
            picked = jnp.sum(terms * mask_ref[b][None], axis=1)
            out_ref[a * 32 : a * 32 + 30, b * 32 : b * 32 + 32] = jnp.dot(
                picked, sum_ref[...], preferred_element_type=F32, precision=lax.Precision.HIGHEST
            )


def grad_kernel(left_ref, *refs):
    panels = panel_places(refs[0:PANELS])
    grad_ref, shift_ref, valid_ref = refs[PANELS : PANELS + 3]
    left_out, right_out = refs[PANELS + 3], refs[PANELS + 4 : PANELS + 11]
    left_rolls, wide, chosen, counts, weights = refs[PANELS + 11 :]
    widen(left_ref, panels, left_rolls, wide)
    row = lax.broadcasted_iota(jnp.int32, (8, 128), 0)
    valid = valid_ref[...].astype(F32)
    shift = shift_ref[...]
    for r in range(8):
        shift_r = rolled(shift, (8 - r) % 8, 0)
        valid_r = rolled(valid, (8 - r) % 8, 0)
        for b in range(BLOCKS):
            q = 6 - b
            at = jnp.where(row <= 7 - r, 8 * q + r, 8 * (q - 1) + r)
            chosen[b, r] = jnp.where(shift_r == at, valid_r, 0.0)
    for b in range(BLOCKS):
        count = chosen[b, 0]
        for r in range(1, 8):
            count = count + chosen[b, r]
        counts[b] = 0.5 * count

    def groups(index, carry):
        pair_rows = pl.ds(pl.multiple_of(index * 16, 16), 16)
        for r in range(8):
            lines = [[], []]
            for q in range(6):
                value = grad_ref[8 * q + r, pair_rows, :].astype(F32)
                for half in range(2):
                    lines[half].append(rolled(value[half * 8 : half * 8 + 8], (8 - r) % 8, 0))
            for half in range(2):
                for b in range(BLOCKS):
                    low = lines[half][6 - b] if b > 0 else 0.0
                    high = lines[half][5 - b] if b < 6 else 0.0
                    mixed = jnp.where(row <= 7 - r, low, high)
                    weights[half, b, r] = mixed * (1.0 / CG) - 0.5 * chosen[b, r]
        base = index * 128
        for half in range(2):
            for b in range(BLOCKS):
                factors = [weights[half, b, r] for r in range(8)]
                count = counts[b]
                for c in range(0, CG, 2):
                    both = []
                    for k in range(2):
                        place = pl.ds(pl.multiple_of(base + half * 64 + (c + k) * 8, 8), 8)
                        acc = count * wide[b, place, :]
                        for r in range(8):
                            acc = acc + factors[r] * left_rolls[r, place, :]
                        both.append(acc)
                    place = pl.ds(pl.multiple_of(base + half * 64 + c * 8, 16), 16)
                    right_out[b][place, :] = jnp.concatenate(both, axis=0).astype(
                        right_out[b].dtype
                    )
            sums = []
            for c in range(CG):
                place = pl.ds(pl.multiple_of(base + half * 64 + c * 8, 8), 8)
                sums.append(0.5 * valid * left_rolls[0, place, :])
            for r in range(8):
                factors = [weights[half, b, r] for b in range(BLOCKS)]
                for c in range(CG):
                    place = pl.ds(pl.multiple_of(base + half * 64 + c * 8, 8), 8)
                    acc = factors[0] * wide[0, place, :]
                    for b in range(1, BLOCKS):
                        acc = acc + factors[b] * wide[b, place, :]
                    sums[c] = sums[c] + rolled(acc, r, 0)
            for c in range(CG):
                place = pl.ds(pl.multiple_of(base + half * 64 + c * 8, 8), 8)
                left_out[place, :] = sums[c]
        return carry

    lax.fori_loop(0, 5, groups, 0)


SMEM = pl.BlockSpec(memory_space=pltpu.SMEM)
VMEM = pl.BlockSpec(memory_space=pltpu.VMEM)
ANY = pl.BlockSpec(memory_space=pl.ANY)


def cost_of(flops, size):
    return pl.CostEstimate(flops=flops, bytes_accessed=size, transcendentals=0)


def run_conv(rank, kernel, slabs):
    return pl.pallas_call(
        conv_kernel,
        out_shape=jax.ShapeDtypeStruct((DISP, 80, 128), BF16),
        in_specs=[SMEM, VMEM] + [ANY] * SLABS,
        out_specs=VMEM,
        scratch_shapes=[pltpu.VMEM((52, ROWS, 128), BF16), pltpu.SemaphoreType.DMA((8,))],
        compiler_params=pltpu.CompilerParams(vmem_limit_bytes=16 * MIB),
        cost_estimate=cost_of(7_000_000_000, 6_000_000),
        name="filter_transpose",
    )(rank, kernel, *slabs)


def run_cost(left, panels):
    return pl.pallas_call(
        cost_kernel,
        out_shape=jax.ShapeDtypeStruct((52, 240, 128), BF16),
        in_specs=[VMEM] * (1 + PANELS),
        out_specs=VMEM,
        scratch_shapes=[
            pltpu.VMEM((8, 640, 128), F32),
            pltpu.VMEM((BLOCKS, 640, 128), F32),
        ],
        compiler_params=pltpu.CompilerParams(vmem_limit_bytes=16 * MIB),
        cost_estimate=cost_of(5_000_000_000, 4_000_000),
        name="cost_volume",
    )(left, *panels)


def picking():
    column, channel = filter_column()
    w = np.arange(8)[None, :, None]
    b = np.arange(3)[:, None, None]
    mask = (w == column[None, None, :] + 2 * b - 2).astype(np.float32)
    summing = (channel[:, None] == np.arange(OUTC)[None]).astype(np.float32)
    return jnp.asarray(mask), jnp.asarray(summing)


def run_filter(rank, volume, slabs):
    return pl.pallas_call(
        filter_kernel,
        out_shape=jax.ShapeDtypeStruct((96, 128), F32),
        in_specs=[SMEM] + [VMEM] * 3 + [ANY] * SLABS,
        out_specs=VMEM,
        scratch_shapes=[
            pltpu.VMEM((DISP, ROWS, 128), BF16),
            pltpu.VMEM((3, 240, ROWS), F32),
            pltpu.SemaphoreType.DMA((8,)),
        ],
        compiler_params=pltpu.CompilerParams(vmem_limit_bytes=20 * MIB),
        cost_estimate=cost_of(8_000_000_000, 4_000_000),
        name="filter_grad",
    )(rank, volume, *picking(), *slabs)


def run_grad(left, panels, grad_cost, shift, valid):
    return pl.pallas_call(
        grad_kernel,
        out_shape=[jax.ShapeDtypeStruct((640, 128), F32)]
        + [jax.ShapeDtypeStruct((640, 128), BF16)] * 6
        + [jax.ShapeDtypeStruct((640, 128), F32)],
        in_specs=[VMEM] * (4 + PANELS),
        out_specs=[VMEM] * 8,
        scratch_shapes=[
            pltpu.VMEM((8, 640, 128), F32),
            pltpu.VMEM((BLOCKS, 640, 128), F32),
            pltpu.VMEM((BLOCKS, 8, 8, 128), F32),
            pltpu.VMEM((BLOCKS, 8, 128), F32),
            pltpu.VMEM((2, BLOCKS, 8, 8, 128), F32),
        ],
        compiler_params=pltpu.CompilerParams(vmem_limit_bytes=24 * MIB),
        cost_estimate=cost_of(5_000_000_000, 4_000_000),
        name="feature_grads",
    )(left, *panels, grad_cost, shift, valid)


def conv_matrix(conv_weight, rank):
    column, channel = filter_column()
    local = lax.dynamic_slice_in_dim(conv_weight, rank * 10, 10, axis=1)
    taps = local.transpose(4, 1, 2, 3, 0)
    spread = (np.arange(OUTC)[:, None] == channel[None]).astype(np.float32)
    placed = jnp.einsum(
        "egabo,oc->egabc", taps, jnp.asarray(spread, BF16), preferred_element_type=BF16
    )
    w = np.arange(8)[None, :, None]
    b = np.arange(3)[:, None, None]
    fits = column[None, None, :] == w - 2 * b + 2
    total = None
    for tap in range(3):
        term = jnp.where(
            jnp.asarray(fits[tap])[None, None, :, None, :], placed[:, :, None, :, tap, :], 0
        )
        total = term if total is None else total + term
    return total.reshape(240, 3 * ROWS).astype(BF16)


def moved(value, axis, place):
    pairs = [(i, place(i)) for i in range(lax.axis_size(axis))]
    return lax.ppermute(value, axis, pairs)


def along(value, steps):
    count = lax.axis_size("lon")
    return moved(value, "lon", lambda i: (i + steps) % count)


def across(value, bits):
    return moved(value, "grp", lambda i: i ^ bits)


def summed_over_lon(value):
    for unit in (1, 4, 16):
        value = value + sum(moved(value, "lon", lambda i: i ^ (unit * k)) for k in (1, 2, 3))
    return value


def together(value, other):
    return lax.optimization_barrier((value, other))[0]


def shards(left_feat, right_feat, conv_cot, conv_weight, disparity_shift, valid_mask):
    rank = lax.axis_index("grp")
    rank_array = rank.astype(jnp.int32).reshape(1)
    right = right_feat.reshape(640, 128)
    left = left_feat.reshape(640, 128)
    own = conv_cot.reshape(12, 256, 128)

    own_far = across(own, 2)
    one = along(jnp.concatenate([right, conv_cot[:, :, 6:].reshape(768, 128)]), 1)
    after = along(conv_cot[:, :, :2].reshape(12, 64, 128), -1)
    halo = jnp.concatenate([one[640:].reshape(12, 64, 128), after], axis=1)
    halo_far = across(halo, 2)
    later = together(right, after)
    two, three, four = (along(later, k) for k in (2, 3, 4))
    pair = along(jnp.concatenate([one[:640], two]), 4)
    panels = [one, two, three, four, pair, right]
    own_later = together(own, after)
    slabs = [own, across(own_later, 1), own_far, across(own_far, 1)]
    slabs += [halo, across(halo, 1), halo_far, across(halo_far, 1)]

    grad_cost = run_conv(rank_array, conv_matrix(conv_weight, rank), slabs)
    volume = run_cost(together(left, grad_cost), panels)
    filter_part = run_filter(rank_array, volume, slabs)
    outs = run_grad(
        together(left, filter_part), panels, grad_cost, disparity_shift, valid_mask
    )
    left_grad = outs[0].reshape(80, 8, 128)
    right_grad = outs[7]
    for k in range(1, 7):
        right_grad = right_grad + along(outs[1 + 6 - k], -k).astype(F32)
    right_grad = right_grad.reshape(80, 8, 128)

    total = summed_over_lon(filter_part)
    pieces = [total] + [across(total, k) for k in range(1, 4)]
    odd, high = (rank & 1) == 1, (rank & 2) == 2
    pieces = [jnp.where(odd, pieces[k ^ 1], pieces[k]) for k in range(4)]
    pieces = [jnp.where(high, pieces[k ^ 2], pieces[k]) for k in range(4)]
    scale = 1.0 / math.sqrt(DISP * 8 * lax.axis_size("lon") * 128)
    whole = jnp.stack(pieces)[:, :, :96].reshape(4, 3, 32, 3, OUTC)[:, :, :30]
    whole = whole.reshape(4, 3, 3, 10, 3, OUTC) * scale
    weight_grad = whole.transpose(5, 0, 3, 1, 4, 2).reshape(OUTC, 40, 3, 3, 3)
    return (left_grad, right_grad, weight_grad)


def solution(mesh):
    placed = (
        P("grp", "lon", None),
        P("grp", "lon", None),
        P("grp", None, "lon", None),
        P(),
        P("lon", None),
        P("lon", None),
    )
    return jax.shard_map(
        shards,
        mesh=mesh,
        in_specs=placed,
        out_specs=(P("grp", "lon", None), P("grp", "lon", None), P()),
        check_vma=False,
    )
```

```python
import functools
import math

import jax
import jax.numpy as jnp
import numpy as np
from jax import lax
from jax.experimental import pallas as pl
from jax.experimental.pallas import tpu as pltpu
from jax.sharding import PartitionSpec as P

CG = 8
DISP = 48
OUTC = 32
COLS_HERE = 8
BLOCKS = 7
ROWS = 384
F32 = jnp.float32
BF16 = jnp.bfloat16
MIB = 1024 * 1024


def filter_column():
    index = np.arange(ROWS)
    own, left = index < 256, index < 320
    column = np.where(own, index % 8, np.where(left, index % 2 - 2, index % 2 + 8))
    channel = np.where(own, index // 8, np.where(left, (index - 256) // 2, (index - 320) // 2))
    return column, channel


SLABS = 8


class PlaneLoad:
    def __init__(self, rank, slabs, planes, first, sems):
        self.copies = []
        for k in range(4):
            place = pl.ds((rank ^ k) * 12 + first, 12)
            for part, (row, rows) in enumerate(((0, 256), (256, 128))):
                self.copies.append(
                    pltpu.make_async_copy(
                        slabs[4 * part + k],
                        planes.at[place, pl.ds(row, rows)],
                        sems.at[4 * part + k],
                    )
                )

    def start(self):
        for copy in self.copies:
            copy.start()

    def wait(self):
        for copy in self.copies:
            copy.wait()


def transposed_filter(kernel_ref, planes, emit, unroll):
    lane = lax.broadcasted_iota(jnp.int32, (80, 128), 1)

    def pair(index, carry):
        d = index * 2
        parts = []
        for a in range(3):
            parts.append(
                jnp.concatenate([planes[d + 4 - 2 * a], planes[d + 5 - 2 * a]], axis=1)
            )
        columns = jnp.concatenate(parts, axis=0)
        product = jnp.dot(kernel_ref[...], columns, preferred_element_type=F32)
        for half in range(2):
            part = product[:, half * 128 : half * 128 + 128]
            ahead = jnp.where(lane < 126, pltpu.roll(part[0:80], 126, 1), 0.0)
            behind = jnp.where(lane >= 2, pltpu.roll(part[160:240], 2, 1), 0.0)
            emit(d + half, part[80:160] + ahead + behind)
        return carry

    lax.fori_loop(0, 24, pair, 0, unroll=unroll)


def conv_kernel(rank_ref, kernel_ref, *refs):
    slabs, (out_ref, planes, sems) = refs[0:SLABS], refs[SLABS:]
    load = PlaneLoad(rank_ref[0], slabs, planes, 2, sems)
    load.start()
    planes[0:2] = jnp.zeros((2, ROWS, 128), BF16)
    planes[50:52] = jnp.zeros((2, ROWS, 128), BF16)
    load.wait()

    def emit(d, value):
        out_ref[d] = value.astype(BF16)

    transposed_filter(kernel_ref, planes, emit, 4)


def rolled(value, steps, axis):
    return value if steps == 0 else pltpu.roll(value, steps, axis)


PANELS = 6


def panel_places(refs):
    one, two, three, four, pair, own = refs
    return [(pair, 640), (pair, 0), (four, 0), (three, 0), (two, 0), (one, 0), (own, 0)]


def widen(left_ref, panels, left_rolls, wide):
    def two(index, carry):
        rows = pl.ds(pl.multiple_of(index * 16, 16), 16)
        value = left_ref[rows, :].astype(F32)
        for half in range(2):
            part = value[half * 8 : half * 8 + 8]
            place = pl.ds(pl.multiple_of(index * 16 + half * 8, 8), 8)
            for r in range(8):
                left_rolls[r, place, :] = rolled(part, (8 - r) % 8, 0)
        for b in range(BLOCKS):
            panel, first = panels[b]
            there = pl.ds(pl.multiple_of(first + index * 16, 16), 16)
            value = panel[there, :].astype(F32)
            wide[b, rows, :] = value
        return carry

    lax.fori_loop(0, 40, two, 0)


def cost_kernel(left_ref, *refs):
    panels = panel_places(refs[0:PANELS])
    volume, left_rolls, wide = refs[PANELS:]
    widen(left_ref, panels, left_rolls, wide)
    volume[0:2] = jnp.zeros((2, 240, 128), BF16)
    volume[50:52] = jnp.zeros((2, 240, 128), BF16)
    row = lax.broadcasted_iota(jnp.int32, (8, 128), 0)
    lane = lax.broadcasted_iota(jnp.int32, (16, 128), 1)

    def groups(index, carry):
        base = index * 128
        for r in range(8):
            sums = []
            for half in range(2):
                line = []
                for b in range(BLOCKS):
                    acc = None
                    for c in range(CG):
                        place = pl.ds(pl.multiple_of(base + half * 64 + c * 8, 8), 8)
                        term = left_rolls[r, place, :] * wide[b, place, :]
                        acc = term if acc is None else acc + term
                    line.append(acc)
                sums.append(line)
            for q in range(6):
                both = []
                for half in range(2):
                    line = sums[half]
                    mixed = jnp.where(row <= 7 - r, line[6 - q], line[5 - q]) if r else line[6 - q]
                    both.append(rolled(mixed, r, 0))
                cost = jnp.concatenate(both, axis=0) * (1.0 / CG)
                d = 8 * q + r
                later = jnp.where(lane >= 2, pltpu.roll(cost, 2, 1), 0.0)
                sooner = jnp.where(lane < 126, pltpu.roll(cost, 126, 1), 0.0)
                for e, value in enumerate((later, cost, sooner)):
                    place = pl.ds(pl.multiple_of(e * 80 + index * 16, 16), 16)
                    volume[d + 2, place, :] = value.astype(BF16)
        return carry

    lax.fori_loop(0, 5, groups, 0)

def filter_kernel(rank_ref, volume, mask_ref, sum_ref, *refs):
    slabs, (out_ref, planes, total, sems) = refs[0:SLABS], refs[SLABS:]
    load = PlaneLoad(rank_ref[0], slabs, planes, 0, sems)
    load.start()
    total[...] = jnp.zeros_like(total)
    load.wait()

    def chunk(index, carry):
        d = index * 16
        cot = jnp.concatenate([planes[d + j] for j in range(16)], axis=1)
        for a in range(3):
            cost = jnp.concatenate([volume[d + j + 2 * a] for j in range(16)], axis=1)
            total[a] += lax.dot_general(
                cost, cot, (((1,), (1,)), ((), ())), preferred_element_type=F32
            )
        return carry

    lax.fori_loop(0, DISP // 16, chunk, 0)
    out_ref[...] = jnp.zeros_like(out_ref)
    for a in range(3):
        terms = total[a].reshape(30, 8, ROWS)
        for b in range(3):
            picked = jnp.sum(terms * mask_ref[b][None], axis=1)
            out_ref[a * 32 : a * 32 + 30, b * 32 : b * 32 + 32] = jnp.dot(
                picked, sum_ref[...], preferred_element_type=F32, precision=lax.Precision.HIGHEST
            )


def grad_kernel(left_ref, *refs):
    panels = panel_places(refs[0:PANELS])
    grad_ref, shift_ref, valid_ref = refs[PANELS : PANELS + 3]
    left_out, right_out = refs[PANELS + 3], refs[PANELS + 4 : PANELS + 11]
    left_rolls, wide, chosen, counts, weights = refs[PANELS + 11 :]
    widen(left_ref, panels, left_rolls, wide)
    row = lax.broadcasted_iota(jnp.int32, (8, 128), 0)
    valid = valid_ref[...].astype(F32)
    shift = shift_ref[...]
    for r in range(8):
        shift_r = rolled(shift, (8 - r) % 8, 0)
        valid_r = rolled(valid, (8 - r) % 8, 0)
        for b in range(BLOCKS):
            q = 6 - b
            at = jnp.where(row <= 7 - r, 8 * q + r, 8 * (q - 1) + r)
            chosen[b, r] = jnp.where(shift_r == at, valid_r, 0.0)
    for b in range(BLOCKS):
        count = chosen[b, 0]
        for r in range(1, 8):
            count = count + chosen[b, r]
        counts[b] = 0.5 * count

    def groups(index, carry):
        pair_rows = pl.ds(pl.multiple_of(index * 16, 16), 16)
        for r in range(8):
            lines = [[], []]
            for q in range(6):
                value = grad_ref[8 * q + r, pair_rows, :].astype(F32)
                for half in range(2):
                    lines[half].append(rolled(value[half * 8 : half * 8 + 8], (8 - r) % 8, 0))
            for half in range(2):
                for b in range(BLOCKS):
                    low = lines[half][6 - b] if b > 0 else 0.0
                    high = lines[half][5 - b] if b < 6 else 0.0
                    mixed = jnp.where(row <= 7 - r, low, high)
                    weights[half, b, r] = mixed * (1.0 / CG) - 0.5 * chosen[b, r]
        base = index * 128
        for half in range(2):
            for b in range(BLOCKS):
                factors = [weights[half, b, r] for r in range(8)]
                count = counts[b]
                for c in range(0, CG, 2):
                    both = []
                    for k in range(2):
                        place = pl.ds(pl.multiple_of(base + half * 64 + (c + k) * 8, 8), 8)
                        acc = count * wide[b, place, :]
                        for r in range(8):
                            acc = acc + factors[r] * left_rolls[r, place, :]
                        both.append(acc)
                    place = pl.ds(pl.multiple_of(base + half * 64 + c * 8, 16), 16)
                    right_out[b][place, :] = jnp.concatenate(both, axis=0).astype(
                        right_out[b].dtype
                    )
            sums = []
            for c in range(CG):
                place = pl.ds(pl.multiple_of(base + half * 64 + c * 8, 8), 8)
                sums.append(0.5 * valid * left_rolls[0, place, :])
            for r in range(8):
                factors = [weights[half, b, r] for b in range(BLOCKS)]
                for c in range(CG):
                    place = pl.ds(pl.multiple_of(base + half * 64 + c * 8, 8), 8)
                    acc = factors[0] * wide[0, place, :]
                    for b in range(1, BLOCKS):
                        acc = acc + factors[b] * wide[b, place, :]
                    sums[c] = sums[c] + rolled(acc, r, 0)
            for c in range(CG):
                place = pl.ds(pl.multiple_of(base + half * 64 + c * 8, 8), 8)
                left_out[place, :] = sums[c]
        return carry

    lax.fori_loop(0, 5, groups, 0)


SMEM = pl.BlockSpec(memory_space=pltpu.SMEM)
VMEM = pl.BlockSpec(memory_space=pltpu.VMEM)
ANY = pl.BlockSpec(memory_space=pl.ANY)


def cost_of(flops, size):
    return pl.CostEstimate(flops=flops, bytes_accessed=size, transcendentals=0)


def run_conv(rank, kernel, slabs):
    return pl.pallas_call(
        conv_kernel,
        out_shape=jax.ShapeDtypeStruct((DISP, 80, 128), BF16),
        in_specs=[SMEM, VMEM] + [ANY] * SLABS,
        out_specs=VMEM,
        scratch_shapes=[pltpu.VMEM((52, ROWS, 128), BF16), pltpu.SemaphoreType.DMA((8,))],
        compiler_params=pltpu.CompilerParams(vmem_limit_bytes=16 * MIB),
        cost_estimate=cost_of(7_000_000_000, 6_000_000),
        name="filter_transpose",
    )(rank, kernel, *slabs)


def run_cost(left, panels):
    return pl.pallas_call(
        cost_kernel,
        out_shape=jax.ShapeDtypeStruct((52, 240, 128), BF16),
        in_specs=[VMEM] * (1 + PANELS),
        out_specs=VMEM,
        scratch_shapes=[
            pltpu.VMEM((8, 640, 128), F32),
            pltpu.VMEM((BLOCKS, 640, 128), F32),
        ],
        compiler_params=pltpu.CompilerParams(vmem_limit_bytes=16 * MIB),
        cost_estimate=cost_of(5_000_000_000, 4_000_000),
        name="cost_volume",
    )(left, *panels)


def picking():
    column, channel = filter_column()
    w = np.arange(8)[None, :, None]
    b = np.arange(3)[:, None, None]
    mask = (w == column[None, None, :] + 2 * b - 2).astype(np.float32)
    summing = (channel[:, None] == np.arange(OUTC)[None]).astype(np.float32)
    return jnp.asarray(mask), jnp.asarray(summing)


def run_filter(rank, volume, slabs):
    return pl.pallas_call(
        filter_kernel,
        out_shape=jax.ShapeDtypeStruct((96, 128), F32),
        in_specs=[SMEM] + [VMEM] * 3 + [ANY] * SLABS,
        out_specs=VMEM,
        scratch_shapes=[
            pltpu.VMEM((DISP, ROWS, 128), BF16),
            pltpu.VMEM((3, 240, ROWS), F32),
            pltpu.SemaphoreType.DMA((8,)),
        ],
        compiler_params=pltpu.CompilerParams(vmem_limit_bytes=20 * MIB),
        cost_estimate=cost_of(8_000_000_000, 4_000_000),
        name="filter_grad",
    )(rank, volume, *picking(), *slabs)


def run_grad(left, panels, grad_cost, shift, valid):
    return pl.pallas_call(
        grad_kernel,
        out_shape=[jax.ShapeDtypeStruct((640, 128), F32)]
        + [jax.ShapeDtypeStruct((640, 128), BF16)] * 6
        + [jax.ShapeDtypeStruct((640, 128), F32)],
        in_specs=[VMEM] * (4 + PANELS),
        out_specs=[VMEM] * 8,
        scratch_shapes=[
            pltpu.VMEM((8, 640, 128), F32),
            pltpu.VMEM((BLOCKS, 640, 128), F32),
            pltpu.VMEM((BLOCKS, 8, 8, 128), F32),
            pltpu.VMEM((BLOCKS, 8, 128), F32),
            pltpu.VMEM((2, BLOCKS, 8, 8, 128), F32),
        ],
        compiler_params=pltpu.CompilerParams(vmem_limit_bytes=24 * MIB),
        cost_estimate=cost_of(5_000_000_000, 4_000_000),
        name="feature_grads",
    )(left, *panels, grad_cost, shift, valid)


def conv_matrix(conv_weight, rank):
    column, channel = filter_column()
    local = lax.dynamic_slice_in_dim(conv_weight, rank * 10, 10, axis=1)
    taps = local.transpose(4, 1, 2, 3, 0)
    spread = (np.arange(OUTC)[:, None] == channel[None]).astype(np.float32)
    placed = jnp.einsum(
        "egabo,oc->egabc", taps, jnp.asarray(spread, BF16), preferred_element_type=BF16
    )
    w = np.arange(8)[None, :, None]
    b = np.arange(3)[:, None, None]
    fits = column[None, None, :] == w - 2 * b + 2
    total = None
    for tap in range(3):
        term = jnp.where(
            jnp.asarray(fits[tap])[None, None, :, None, :], placed[:, :, None, :, tap, :], 0
        )
        total = term if total is None else total + term
    return total.reshape(240, 3 * ROWS).astype(BF16)


def moved(value, axis, place):
    pairs = [(i, place(i)) for i in range(lax.axis_size(axis))]
    return lax.ppermute(value, axis, pairs)


def along(value, steps):
    count = lax.axis_size("lon")
    return moved(value, "lon", lambda i: (i + steps) % count)


def across(value, bits):
    return moved(value, "grp", lambda i: i ^ bits)


def together(value, other):
    return lax.optimization_barrier((value, other))[0]


def summed_over_lon(value, gates):
    for unit, gate in zip((1, 4, 16), gates):
        parts = [moved(value, "lon", lambda i: i ^ (unit * k)) for k in (1, 2, 3)]
        value = value + parts[0] + parts[1] + parts[2]
        if gate is not None:
            value = together(value, gate)
    return value


def shards(left_feat, right_feat, conv_cot, conv_weight, disparity_shift, valid_mask):
    rank = lax.axis_index("grp")
    rank_array = rank.astype(jnp.int32).reshape(1)
    right = right_feat.reshape(640, 128)
    left = left_feat.reshape(640, 128)
    own = conv_cot.reshape(12, 256, 128)

    own_far = across(own, 2)
    one = along(jnp.concatenate([right, conv_cot[:, :, 6:].reshape(768, 128)]), 1)
    after = along(conv_cot[:, :, :2].reshape(12, 64, 128), -1)
    halo = jnp.concatenate([one[640:].reshape(12, 64, 128), after], axis=1)
    halo_far = across(halo, 2)
    later = together(right, after)
    two, three, four = (along(later, k) for k in (2, 3, 4))
    pair = along(jnp.concatenate([one[:640], two]), 4)
    panels = [one, two, three, four, pair, right]
    own_later = together(own, after)
    slabs = [own, across(own_later, 1), own_far, across(own_far, 1)]
    slabs += [halo, across(halo, 1), halo_far, across(halo_far, 1)]

    grad_cost = run_conv(rank_array, conv_matrix(conv_weight, rank), slabs)
    volume = run_cost(together(left, grad_cost), panels)
    filter_part = run_filter(rank_array, volume, slabs)
    outs = run_grad(together(left, filter_part), panels, grad_cost, disparity_shift, valid_mask)
    left_grad = outs[0].reshape(80, 8, 128)
    back = {k: along(outs[7 - k], -k) for k in (6, 5, 4, 3, 2, 1)}
    right_grad = outs[7]
    for k in range(1, 7):
        right_grad = right_grad + back[k].astype(F32)
    right_grad = right_grad.reshape(80, 8, 128)
    total = summed_over_lon(filter_part, (outs[7], None, None))

    pieces = [total] + [across(total, k) for k in range(1, 4)]
    odd, high = (rank & 1) == 1, (rank & 2) == 2
    pieces = [jnp.where(odd, pieces[k ^ 1], pieces[k]) for k in range(4)]
    pieces = [jnp.where(high, pieces[k ^ 2], pieces[k]) for k in range(4)]
    scale = 1.0 / math.sqrt(DISP * 8 * lax.axis_size("lon") * 128)
    whole = jnp.stack(pieces)[:, :, :96].reshape(4, 3, 32, 3, OUTC)[:, :, :30]
    whole = whole.reshape(4, 3, 3, 10, 3, OUTC) * scale
    weight_grad = whole.transpose(5, 0, 3, 1, 4, 2).reshape(OUTC, 40, 3, 3, 3)
    return (left_grad, right_grad, weight_grad)


def solution(mesh):
    placed = (
        P("grp", "lon", None),
        P("grp", "lon", None),
        P("grp", None, "lon", None),
        P(),
        P("lon", None),
        P("lon", None),
    )
    return jax.shard_map(
        shards,
        mesh=mesh,
        in_specs=placed,
        out_specs=(P("grp", "lon", None), P("grp", "lon", None), P()),
        check_vma=False,
    )
```

```python
import functools
import math

import jax
import jax.numpy as jnp
import numpy as np
from jax import lax
from jax.experimental import pallas as pl
from jax.experimental.pallas import tpu as pltpu
from jax.sharding import PartitionSpec as P

CG = 8
DISP = 48
OUTC = 32
COLS_HERE = 8
BLOCKS = 7
ROWS = 384
F32 = jnp.float32
BF16 = jnp.bfloat16
MIB = 1024 * 1024


def filter_column():
    index = np.arange(ROWS)
    own, left = index < 256, index < 320
    column = np.where(own, index % 8, np.where(left, index % 2 - 2, index % 2 + 8))
    channel = np.where(own, index // 8, np.where(left, (index - 256) // 2, (index - 320) // 2))
    return column, channel


SLABS = 8


class PlaneLoad:
    def __init__(self, rank, slabs, planes, first, sems):
        self.copies = []
        for k in range(4):
            place = pl.ds((rank ^ k) * 12 + first, 12)
            for part, (row, rows) in enumerate(((0, 256), (256, 128))):
                self.copies.append(
                    pltpu.make_async_copy(
                        slabs[4 * part + k],
                        planes.at[place, pl.ds(row, rows)],
                        sems.at[4 * part + k],
                    )
                )

    def start(self):
        for copy in self.copies:
            copy.start()

    def wait(self):
        for copy in self.copies:
            copy.wait()


def transposed_filter(kernel_ref, planes, emit, unroll):
    lane = lax.broadcasted_iota(jnp.int32, (80, 128), 1)

    def pair(index, carry):
        d = index * 2
        parts = []
        for a in range(3):
            parts.append(
                jnp.concatenate([planes[d + 4 - 2 * a], planes[d + 5 - 2 * a]], axis=1)
            )
        columns = jnp.concatenate(parts, axis=0)
        product = jnp.dot(kernel_ref[...], columns, preferred_element_type=F32)
        for half in range(2):
            part = product[:, half * 128 : half * 128 + 128]
            ahead = jnp.where(lane < 126, pltpu.roll(part[0:80], 126, 1), 0.0)
            behind = jnp.where(lane >= 2, pltpu.roll(part[160:240], 2, 1), 0.0)
            emit(d + half, part[80:160] + ahead + behind)
        return carry

    lax.fori_loop(0, 24, pair, 0, unroll=unroll)


def conv_kernel(rank_ref, kernel_ref, *refs):
    slabs, (out_ref, planes, sems) = refs[0:SLABS], refs[SLABS:]
    load = PlaneLoad(rank_ref[0], slabs, planes, 2, sems)
    load.start()
    planes[0:2] = jnp.zeros((2, ROWS, 128), BF16)
    planes[50:52] = jnp.zeros((2, ROWS, 128), BF16)
    load.wait()

    def emit(d, value):
        out_ref[d] = value.astype(BF16)

    transposed_filter(kernel_ref, planes, emit, 4)


def rolled(value, steps, axis):
    return value if steps == 0 else pltpu.roll(value, steps, axis)


PANELS = 6


def panel_places(refs):
    one, two, three, four, pair, own = refs
    return [(pair, 640), (pair, 0), (four, 0), (three, 0), (two, 0), (one, 0), (own, 0)]


def widen(left_ref, panels, left_rolls, wide):
    def two(index, carry):
        rows = pl.ds(pl.multiple_of(index * 16, 16), 16)
        value = left_ref[rows, :].astype(F32)
        for half in range(2):
            part = value[half * 8 : half * 8 + 8]
            place = pl.ds(pl.multiple_of(index * 16 + half * 8, 8), 8)
            for r in range(8):
                left_rolls[r, place, :] = rolled(part, (8 - r) % 8, 0)
        for b in range(BLOCKS):
            panel, first = panels[b]
            there = pl.ds(pl.multiple_of(first + index * 16, 16), 16)
            value = panel[there, :].astype(F32)
            wide[b, rows, :] = value
        return carry

    lax.fori_loop(0, 40, two, 0)


def cost_kernel(left_ref, *refs):
    panels = panel_places(refs[0:PANELS])
    volume, left_rolls, wide = refs[PANELS:]
    widen(left_ref, panels, left_rolls, wide)
    volume[0:2] = jnp.zeros((2, 240, 128), BF16)
    volume[50:52] = jnp.zeros((2, 240, 128), BF16)
    row = lax.broadcasted_iota(jnp.int32, (8, 128), 0)
    lane = lax.broadcasted_iota(jnp.int32, (16, 128), 1)

    def groups(index, carry):
        base = index * 128
        for r in range(8):
            sums = []
            for half in range(2):
                line = []
                for b in range(BLOCKS):
                    acc = None
                    for c in range(CG):
                        place = pl.ds(pl.multiple_of(base + half * 64 + c * 8, 8), 8)
                        term = left_rolls[r, place, :] * wide[b, place, :]
                        acc = term if acc is None else acc + term
                    line.append(acc)
                sums.append(line)
            for q in range(6):
                both = []
                for half in range(2):
                    line = sums[half]
                    mixed = jnp.where(row <= 7 - r, line[6 - q], line[5 - q]) if r else line[6 - q]
                    both.append(rolled(mixed, r, 0))
                cost = jnp.concatenate(both, axis=0) * (1.0 / CG)
                d = 8 * q + r
                later = jnp.where(lane >= 2, pltpu.roll(cost, 2, 1), 0.0)
                sooner = jnp.where(lane < 126, pltpu.roll(cost, 126, 1), 0.0)
                for e, value in enumerate((later, cost, sooner)):
                    place = pl.ds(pl.multiple_of(e * 80 + index * 16, 16), 16)
                    volume[d + 2, place, :] = value.astype(BF16)
        return carry

    lax.fori_loop(0, 5, groups, 0)

def filter_kernel(rank_ref, volume, mask_ref, sum_ref, *refs):
    slabs, (out_ref, planes, total, sems) = refs[0:SLABS], refs[SLABS:]
    load = PlaneLoad(rank_ref[0], slabs, planes, 0, sems)
    load.start()
    total[...] = jnp.zeros_like(total)
    load.wait()

    def chunk(index, carry):
        d = index * 16
        cot = jnp.concatenate([planes[d + j] for j in range(16)], axis=1)
        for a in range(3):
            cost = jnp.concatenate([volume[d + j + 2 * a] for j in range(16)], axis=1)
            total[a] += lax.dot_general(
                cost, cot, (((1,), (1,)), ((), ())), preferred_element_type=F32
            )
        return carry

    lax.fori_loop(0, DISP // 16, chunk, 0)
    out_ref[...] = jnp.zeros_like(out_ref)
    for a in range(3):
        terms = total[a].reshape(30, 8, ROWS)
        for b in range(3):
            picked = jnp.sum(terms * mask_ref[b][None], axis=1)
            out_ref[a * 32 : a * 32 + 30, b * 32 : b * 32 + 32] = jnp.dot(
                picked, sum_ref[...], preferred_element_type=F32, precision=lax.Precision.HIGHEST
            )


def grad_kernel(left_ref, *refs):
    panels = panel_places(refs[0:PANELS])
    grad_ref, shift_ref, valid_ref = refs[PANELS : PANELS + 3]
    left_out, right_out = refs[PANELS + 3], refs[PANELS + 4 : PANELS + 11]
    left_rolls, wide, chosen, counts, weights = refs[PANELS + 11 :]
    widen(left_ref, panels, left_rolls, wide)
    row = lax.broadcasted_iota(jnp.int32, (8, 128), 0)
    valid = valid_ref[...].astype(F32)
    shift = shift_ref[...]
    for r in range(8):
        shift_r = rolled(shift, (8 - r) % 8, 0)
        valid_r = rolled(valid, (8 - r) % 8, 0)
        for b in range(BLOCKS):
            q = 6 - b
            at = jnp.where(row <= 7 - r, 8 * q + r, 8 * (q - 1) + r)
            chosen[b, r] = jnp.where(shift_r == at, valid_r, 0.0)
    for b in range(BLOCKS):
        count = chosen[b, 0]
        for r in range(1, 8):
            count = count + chosen[b, r]
        counts[b] = 0.5 * count

    def groups(index, carry):
        pair_rows = pl.ds(pl.multiple_of(index * 16, 16), 16)
        for r in range(8):
            lines = [[], []]
            for q in range(6):
                value = grad_ref[8 * q + r, pair_rows, :].astype(F32)
                for half in range(2):
                    lines[half].append(rolled(value[half * 8 : half * 8 + 8], (8 - r) % 8, 0))
            for half in range(2):
                for b in range(BLOCKS):
                    low = lines[half][6 - b] if b > 0 else 0.0
                    high = lines[half][5 - b] if b < 6 else 0.0
                    mixed = jnp.where(row <= 7 - r, low, high)
                    weights[half, b, r] = mixed * (1.0 / CG) - 0.5 * chosen[b, r]
        base = index * 128
        for half in range(2):
            for b in range(BLOCKS):
                factors = [weights[half, b, r] for r in range(8)]
                count = counts[b]
                for c in range(0, CG, 2):
                    both = []
                    for k in range(2):
                        place = pl.ds(pl.multiple_of(base + half * 64 + (c + k) * 8, 8), 8)
                        acc = count * wide[b, place, :]
                        for r in range(8):
                            acc = acc + factors[r] * left_rolls[r, place, :]
                        both.append(acc)
                    place = pl.ds(pl.multiple_of(base + half * 64 + c * 8, 16), 16)
                    right_out[b][place, :] = jnp.concatenate(both, axis=0).astype(
                        right_out[b].dtype
                    )
            sums = []
            for c in range(CG):
                place = pl.ds(pl.multiple_of(base + half * 64 + c * 8, 8), 8)
                sums.append(0.5 * valid * left_rolls[0, place, :])
            for r in range(8):
                factors = [weights[half, b, r] for b in range(BLOCKS)]
                for c in range(CG):
                    place = pl.ds(pl.multiple_of(base + half * 64 + c * 8, 8), 8)
                    acc = factors[0] * wide[0, place, :]
                    for b in range(1, BLOCKS):
                        acc = acc + factors[b] * wide[b, place, :]
                    sums[c] = sums[c] + rolled(acc, r, 0)
            for c in range(CG):
                place = pl.ds(pl.multiple_of(base + half * 64 + c * 8, 8), 8)
                left_out[place, :] = sums[c]
        return carry

    lax.fori_loop(0, 5, groups, 0)


SMEM = pl.BlockSpec(memory_space=pltpu.SMEM)
VMEM = pl.BlockSpec(memory_space=pltpu.VMEM)
ANY = pl.BlockSpec(memory_space=pl.ANY)


def cost_of(flops, size):
    return pl.CostEstimate(flops=flops, bytes_accessed=size, transcendentals=0)


def run_conv(rank, kernel, slabs):
    return pl.pallas_call(
        conv_kernel,
        out_shape=jax.ShapeDtypeStruct((DISP, 80, 128), BF16),
        in_specs=[SMEM, VMEM] + [ANY] * SLABS,
        out_specs=VMEM,
        scratch_shapes=[pltpu.VMEM((52, ROWS, 128), BF16), pltpu.SemaphoreType.DMA((8,))],
        compiler_params=pltpu.CompilerParams(vmem_limit_bytes=16 * MIB),
        cost_estimate=cost_of(7_000_000_000, 6_000_000),
        name="filter_transpose",
    )(rank, kernel, *slabs)


def run_cost(left, panels):
    return pl.pallas_call(
        cost_kernel,
        out_shape=jax.ShapeDtypeStruct((52, 240, 128), BF16),
        in_specs=[VMEM] * (1 + PANELS),
        out_specs=VMEM,
        scratch_shapes=[
            pltpu.VMEM((8, 640, 128), F32),
            pltpu.VMEM((BLOCKS, 640, 128), F32),
        ],
        compiler_params=pltpu.CompilerParams(vmem_limit_bytes=16 * MIB),
        cost_estimate=cost_of(5_000_000_000, 4_000_000),
        name="cost_volume",
    )(left, *panels)


def picking():
    column, channel = filter_column()
    w = np.arange(8)[None, :, None]
    b = np.arange(3)[:, None, None]
    mask = (w == column[None, None, :] + 2 * b - 2).astype(np.float32)
    summing = (channel[:, None] == np.arange(OUTC)[None]).astype(np.float32)
    return jnp.asarray(mask), jnp.asarray(summing)


def run_filter(rank, volume, slabs):
    return pl.pallas_call(
        filter_kernel,
        out_shape=jax.ShapeDtypeStruct((96, 128), F32),
        in_specs=[SMEM] + [VMEM] * 3 + [ANY] * SLABS,
        out_specs=VMEM,
        scratch_shapes=[
            pltpu.VMEM((DISP, ROWS, 128), BF16),
            pltpu.VMEM((3, 240, ROWS), F32),
            pltpu.SemaphoreType.DMA((8,)),
        ],
        compiler_params=pltpu.CompilerParams(vmem_limit_bytes=20 * MIB),
        cost_estimate=cost_of(8_000_000_000, 4_000_000),
        name="filter_grad",
    )(rank, volume, *picking(), *slabs)


def run_grad(left, panels, grad_cost, shift, valid):
    return pl.pallas_call(
        grad_kernel,
        out_shape=[jax.ShapeDtypeStruct((640, 128), F32)]
        + [jax.ShapeDtypeStruct((640, 128), BF16)] * 6
        + [jax.ShapeDtypeStruct((640, 128), F32)],
        in_specs=[VMEM] * (4 + PANELS),
        out_specs=[VMEM] * 8,
        scratch_shapes=[
            pltpu.VMEM((8, 640, 128), F32),
            pltpu.VMEM((BLOCKS, 640, 128), F32),
            pltpu.VMEM((BLOCKS, 8, 8, 128), F32),
            pltpu.VMEM((BLOCKS, 8, 128), F32),
            pltpu.VMEM((2, BLOCKS, 8, 8, 128), F32),
        ],
        compiler_params=pltpu.CompilerParams(vmem_limit_bytes=24 * MIB),
        cost_estimate=cost_of(5_000_000_000, 4_000_000),
        name="feature_grads",
    )(left, *panels, grad_cost, shift, valid)


def conv_matrix(conv_weight, rank):
    column, channel = filter_column()
    local = lax.dynamic_slice_in_dim(conv_weight, rank * 10, 10, axis=1)
    taps = local.transpose(4, 1, 2, 3, 0)
    spread = (np.arange(OUTC)[:, None] == channel[None]).astype(np.float32)
    placed = jnp.einsum(
        "egabo,oc->egabc", taps, jnp.asarray(spread, BF16), preferred_element_type=BF16
    )
    w = np.arange(8)[None, :, None]
    b = np.arange(3)[:, None, None]
    fits = column[None, None, :] == w - 2 * b + 2
    total = None
    for tap in range(3):
        term = jnp.where(
            jnp.asarray(fits[tap])[None, None, :, None, :], placed[:, :, None, :, tap, :], 0
        )
        total = term if total is None else total + term
    return total.reshape(240, 3 * ROWS).astype(BF16)


def moved(value, axis, place):
    pairs = [(i, place(i)) for i in range(lax.axis_size(axis))]
    return lax.ppermute(value, axis, pairs)


def along(value, steps):
    count = lax.axis_size("lon")
    return moved(value, "lon", lambda i: (i + steps) % count)


def across(value, bits):
    return moved(value, "grp", lambda i: i ^ bits)


def together(value, other):
    return lax.optimization_barrier((value, other))[0]


def summed_over_lon(value, gates):
    for unit, gate in zip((1, 4, 16), gates):
        parts = [moved(value, "lon", lambda i: i ^ (unit * k)) for k in (1, 2, 3)]
        value = value + parts[0] + parts[1] + parts[2]
        if gate is not None:
            value = together(value, gate)
    return value


def shards(left_feat, right_feat, conv_cot, conv_weight, disparity_shift, valid_mask):
    rank = lax.axis_index("grp")
    rank_array = rank.astype(jnp.int32).reshape(1)
    right = right_feat.reshape(640, 128)
    left = left_feat.reshape(640, 128)
    own = conv_cot.reshape(12, 256, 128)

    own_far = across(own, 2)
    one = along(jnp.concatenate([right, conv_cot[:, :, 6:].reshape(768, 128)]), 1)
    after = along(conv_cot[:, :, :2].reshape(12, 64, 128), -1)
    halo = jnp.concatenate([one[640:].reshape(12, 64, 128), after], axis=1)
    halo_far = across(halo, 2)
    later = together(right, after)
    two, three, four = along(right, 2), along(later, 3), along(later, 4)
    pair = along(jnp.concatenate([one[:640], two]), 4)
    panels = [one, two, three, four, pair, right]
    own_later = together(own, after)
    slabs = [own, across(own_later, 1), own_far, across(own_far, 1)]
    slabs += [halo, across(halo, 1), halo_far, across(halo_far, 1)]

    grad_cost = run_conv(rank_array, conv_matrix(conv_weight, rank), slabs)
    volume = run_cost(together(left, grad_cost), panels)
    filter_part = run_filter(rank_array, volume, slabs)
    outs = run_grad(together(left, filter_part), panels, grad_cost, disparity_shift, valid_mask)
    left_grad = outs[0].reshape(80, 8, 128)
    back = {k: along(outs[7 - k], -k) for k in (6, 5, 4, 3, 2, 1)}
    right_grad = outs[7]
    for k in range(1, 7):
        right_grad = right_grad + back[k].astype(F32)
    right_grad = right_grad.reshape(80, 8, 128)
    total = summed_over_lon(filter_part, (outs[7], None, None))

    pieces = [total] + [across(total, k) for k in range(1, 4)]
    odd, high = (rank & 1) == 1, (rank & 2) == 2
    pieces = [jnp.where(odd, pieces[k ^ 1], pieces[k]) for k in range(4)]
    pieces = [jnp.where(high, pieces[k ^ 2], pieces[k]) for k in range(4)]
    scale = 1.0 / math.sqrt(DISP * 8 * lax.axis_size("lon") * 128)
    whole = jnp.stack(pieces)[:, :, :96].reshape(4, 3, 32, 3, OUTC)[:, :, :30]
    whole = whole.reshape(4, 3, 3, 10, 3, OUTC) * scale
    weight_grad = whole.transpose(5, 0, 3, 1, 4, 2).reshape(OUTC, 40, 3, 3, 3)
    return (left_grad, right_grad, weight_grad)


def solution(mesh):
    placed = (
        P("grp", "lon", None),
        P("grp", "lon", None),
        P("grp", None, "lon", None),
        P(),
        P("lon", None),
        P("lon", None),
    )
    return jax.shard_map(
        shards,
        mesh=mesh,
        in_specs=placed,
        out_specs=(P("grp", "lon", None), P("grp", "lon", None), P()),
        check_vma=False,
    )
```
